32 devices in a mesh: slab: 32 (over z, y, x, core).
Axes of the slice: x: 2, y: 2, z: 4, core: 2. Of those that a mesh axis runs over, the one named last changes fastest.
Arguments:
- velocity: bfloat16 [3, 128, 16, 4096], P(None, 'slab'), may hold values from -6 to 6
Outputs:
- composite: float32 [4, 32768], P(None, 'slab')
The draws below stay inside these ranges and needn't reach their ends.
All inputs are finite; a program needn't handle non-finite values.
Results may differ from the reference program's by a relative error of at most 0.00085.
Values may be sent and summed in bfloat16 or wider, within the bound.
A program may use at most 192 MiB of HBM per device.

```python
import jax
import jax.numpy as jnp
from jax import lax

CZ = 4
BAND = 8
NX = 4096
YH = 16
NZ = 128
N_SLAB = 32


def steps_of(rng, dims, split, low, high):
    loudness, own = 1.0, jax.random.fold_in(rng, 6)
    for dim, shards_of in split:
        heights = jnp.exp(jax.random.uniform(jax.random.fold_in(own, dim), (shards_of,), jnp.float32, low / len(split), high / len(split)))
        loudness = loudness * jnp.repeat(heights, dims[dim] // shards_of).reshape([-1 if axis == dim else 1 for axis in range(len(dims))])
    return loudness


def bell_draw(key, extent, deviation, most, cuts=(), kind=jnp.bfloat16):
    level = steps_of(key, extent, cuts, -0.22, 0.18) if cuts else 1.0
    result = jax.random.normal(key, extent, jnp.float32) * deviation * level
    return jnp.minimum(jnp.maximum(result, -most), most).astype(kind)


def setup_inputs(seed: int = 0) -> dict:
    key_of = jax.random.split(jax.random.key(seed), 2)
    velocity = bell_draw(key_of[0], (3, NZ, YH, NX), 1.0, 6.0, ((1, 32),))
    return {"velocity": velocity}


taps = (1.0 / 16.0, 4.0 / 16.0, 6.0 / 16.0, 4.0 / 16.0, 1.0 / 16.0)
opacity_gain = 5.0
colour_gain = 2.0


def smooth_valid(field, along):
    length = field.shape[along]
    total = taps[0] * lax.slice_in_dim(field, 0, length - 4, axis=along)
    for offset in range(1, 5):
        total = total + taps[offset] * lax.slice_in_dim(field, offset, length - 4 + offset, axis=along)
    return total


def smooth_wrap(field, along):
    total = taps[0] * jnp.roll(field, 2, along)
    for offset in range(1, 5):
        total = total + taps[offset] * jnp.roll(field, 2 - offset, along)
    return total


def derive_valid(field, along):
    length = field.shape[along]
    first = lax.slice_in_dim(field, 0, length - 4, axis=along)
    second = lax.slice_in_dim(field, 1, length - 3, axis=along)
    fourth = lax.slice_in_dim(field, 3, length - 1, axis=along)
    fifth = lax.slice_in_dim(field, 4, length, axis=along)
    return (first - 8.0 * second + 8.0 * fourth - fifth) / 12.0


def derive_wrap(field, along):
    return (jnp.roll(field, 2, along) - 8.0 * jnp.roll(field, 1, along) + 8.0 * jnp.roll(field, -1, along) - jnp.roll(field, -2, along)) / 12.0


def slab_image(smoothed, planes_total):
    comp_x = smoothed[0]
    comp_y = smoothed[1]
    comp_z = smoothed[2]

    def along_z(field):
        return derive_valid(field, 0)[:, 2:-2]

    def along_y(field):
        return derive_valid(field[2:-2], 1)

    def along_x(field):
        return derive_wrap(field[2:-2, 2:-2], 2)

    curl_x = along_y(comp_z) - along_z(comp_y)
    curl_y = along_z(comp_x) - along_x(comp_z)
    curl_z = along_x(comp_y) - along_y(comp_x)
    density = opacity_gain * (curl_x * curl_x + curl_y * curl_y + curl_z * curl_z) / planes_total
    colour = jax.nn.sigmoid(colour_gain * smoothed[:, 2:-2, 2:-2])
    running = jnp.cumsum(density, axis=0)
    before = jnp.concatenate([jnp.zeros_like(density[:1]), running[:-1]], axis=0)
    weight = jnp.exp(-before) * (1.0 - jnp.exp(-density))
    colour_sum = jnp.sum(weight[None] * colour, axis=1)
    colour_sum = colour_sum.reshape(3, -1)
    depth = jnp.sum(density, axis=0).reshape(-1)
    return colour_sum, depth


def reference(velocity):
    def step(carry, block):
        colour_acc, depth_acc = carry
        start = block * CZ
        planes = (start - 4 + jnp.arange(CZ + 8, dtype=jnp.int32)) % NZ
        piece = jnp.take(velocity, planes.astype(jnp.int32), axis=1).astype(jnp.float32)
        smoothed = smooth_wrap(smooth_valid(smooth_valid(piece, 1), 2), 3)
        colour_part, depth_part = slab_image(smoothed, NZ)
        colour_acc = colour_acc + jnp.exp(-depth_acc)[None] * colour_part
        depth_acc = depth_acc + depth_part
        return (colour_acc, depth_acc), None

    start_colour = jnp.zeros((3, BAND * NX), jnp.float32)
    start_depth = jnp.zeros((BAND * NX,), jnp.float32)
    (colour_acc, depth_acc), unused = lax.scan(step, (start_colour, start_depth), jnp.arange(N_SLAB, dtype=jnp.int32))
    return jnp.concatenate([colour_acc, (1.0 - jnp.exp(-depth_acc))[None]], axis=0)
```

```python
import functools

import jax
import jax.numpy as jnp
import ml_dtypes
import numpy as np
from jax import lax
from jax.experimental import pallas as pl
from jax.experimental.pallas import tpu as pltpu
from jax.sharding import PartitionSpec as P

MESH = pl.DeviceIdType.MESH
opacity_gain = 5.0

smooth_taps = np.array([1, 4, 6, 4, 1]) / 16.0
slope_taps = np.array([1, -8, 0, 8, -1]) / 1.0
both_taps = np.convolve(smooth_taps, slope_taps)
CZ, YH, BAND = 4, 16, 8
KEEP = YH - 4
FIELDS = 6
LANE = 128
SIDE = 96
MARGIN = 256
CHUNK = 1024


def halo_row(component, plane, row):
    below = plane < 0
    source = plane + CZ if below else plane - CZ
    spec, band = (0, 32) if below else (SIDE + 64, SIDE)
    near = source - 2 if below else source
    if component < 2 and 2 <= row < 2 + BAND:
        return band + 32 * component + source * BAND + row - 2
    assert component != 1 and 0 <= near < 2
    if component == 0:
        return spec + near * 4 + (row if row < 2 else row - BAND)
    return spec + 8 + near * KEEP + row


def weights():
    send = np.zeros((128, 192))
    own = np.zeros((FIELDS * 32, 192))
    halo = np.zeros((FIELDS * 32, 192))

    def put(at, component, source, row):
        for b in range(5):
            send[at, component * 64 + source * YH + row + b] += smooth_taps[b]

    for component in range(2):
        for source in range(CZ):
            for r in range(BAND):
                put(32 + 32 * component + source * BAND + r, component, source, r + 2)
    for start, planes in ((0, (2, 3)), (96, (0, 1))):
        for near, source in enumerate(planes):
            for i, row in enumerate((0, 1, 10, 11)):
                put(start + near * 4 + i, 0, source, row)
            for row in range(KEEP):
                put(start + 8 + near * KEEP + row, 2, source, row)

    def term(field, component, z_taps, y_slope, sign):
        y_own = both_taps if y_slope else smooth_taps
        y_halo = slope_taps if y_slope else np.ones(1)
        for p in range(CZ):
            for r in range(BAND):
                at = field * 32 + p * BAND + r
                for a, wz in enumerate(z_taps):
                    plane = p + a - len(z_taps) // 2
                    if wz == 0:
                        continue
                    if 0 <= plane < CZ:
                        for b, wy in enumerate(y_own):
                            row = r + 4 + b - len(y_own) // 2
                            own[at, component * 64 + plane * YH + row] += sign * wz * wy / 16.0
                    else:
                        for b, wy in enumerate(y_halo):
                            if wy:
                                row = r + 2 + b - len(y_halo) // 2
                                halo[at, halo_row(component, plane, row)] += sign * wz * wy / 16.0

    term(0, 2, smooth_taps, True, 1.0)
    term(0, 1, both_taps, False, -1.0)
    term(1, 0, both_taps, False, 1.0)
    term(2, 0, smooth_taps, True, 1.0)
    for k in range(3):
        term(3 + k, k, smooth_taps, False, 1.0)
    full = np.concatenate([send, own, halo], axis=0)
    rounded = full.astype(ml_dtypes.bfloat16)
    assert np.all(rounded.astype(np.float64) == full)
    return rounded


def shift(field, by):
    return pltpu.roll(field, by % field.shape[1], 1)


def smooth_x(field):
    for _ in range(2):
        field = field + shift(field, 1)
        field = field + shift(field, -1)
    return field


def slope_x(field):
    near = shift(field, -1) - shift(field, 1)
    return 8.0 * near - (shift(near, 1) + shift(near, -1))


def spans(nx):
    chunks = nx // CHUNK
    cuts = [[(nx - MARGIN, MARGIN), (0, CHUNK + MARGIN)]]
    for c in range(1, chunks):
        first = c * CHUNK + MARGIN
        cuts.append([(first, min(CHUNK, nx - MARGIN - first))])
    return cuts


def kernel(n, exchange, nx, raw, mats, out, send, halo, fields, *rest):
    if exchange:
        staged, outbox, inbox, up_s, up_r, down_s, down_r, out_s, in_r = rest
    else:
        up_s, up_r, down_s, down_r = rest
    me = lax.axis_index("slab")
    up, down = lax.rem(me + 1, n), lax.rem(me + n - 1, n)
    barrier = pltpu.get_barrier_semaphore()
    cuts = spans(nx)
    pieces = [(c, i, first, width) for c, cut in enumerate(cuts) for i, (first, width) in enumerate(cut)]
    number = {(c, i): k for k, (c, i, _, _) in enumerate(pieces)}

    if exchange:
        def greet(hop, _):
            pl.semaphore_signal(barrier, inc=1, device_id=(lax.rem(me + hop, n),), device_id_type=MESH)
            return 0

        lax.fori_loop(1, n, greet, 0)
    else:
        for other in (up, down):
            pl.semaphore_signal(barrier, inc=1, device_id=(other,), device_id_type=MESH)

    def halo_copies(k):
        _, _, first, width = pieces[k]
        lanes = pl.ds(first, width)
        return (
            pltpu.make_async_remote_copy(
                src_ref=send.at[pl.ds(0, SIDE), lanes], dst_ref=halo.at[pl.ds(0, SIDE), lanes],
                send_sem=up_s.at[k], recv_sem=up_r.at[k], device_id=(up,), device_id_type=MESH),
            pltpu.make_async_remote_copy(
                src_ref=send.at[pl.ds(32, SIDE), lanes], dst_ref=halo.at[pl.ds(SIDE, SIDE), lanes],
                send_sem=down_s.at[k], recv_sem=down_r.at[k], device_id=(down,), device_id_type=MESH),
        )

    for k, (_, _, first, width) in enumerate(pieces):
        send[:, pl.ds(first, width)] = jnp.dot(
            mats[0:128, :], raw[:, pl.ds(first, width)], preferred_element_type=jnp.float32
        ).astype(jnp.bfloat16)
        if k == 0:
            pl.semaphore_wait(barrier, n - 1 if exchange else 2)
        for copy in halo_copies(k):
            copy.start()

    def places(first, width):
        here = [(first + MARGIN, 0, width)]
        if first == 0:
            here.append((nx + MARGIN, 0, MARGIN))
        if first + width == nx:
            here.append((0, width - MARGIN, MARGIN))
        return here

    for _, _, first, width in pieces:
        own = jnp.dot(mats[128:320, :], raw[:, pl.ds(first, width)], preferred_element_type=jnp.float32)
        fields[:, pl.ds(first + MARGIN, width)] = own

    def add_halo(first, width):
        more = jnp.dot(mats[320:512, :], halo[:, pl.ds(first, width)], preferred_element_type=jnp.float32)
        total = fields[:, pl.ds(first + MARGIN, width)] + more
        for at, skip, size in places(first, width):
            fields[:, pl.ds(at, size)] = total[:, skip:skip + size]

    scale = opacity_gain / (144.0 * CZ * n)
    for c, cut in enumerate(cuts):
        for i, (first, width) in enumerate(cut):
            for copy in halo_copies(number[(c, i)]):
                copy.wait_recv()
            add_halo(first, width)
        begin = MARGIN + c * CHUNK - LANE
        window = pl.ds(begin, CHUNK + 2 * LANE)

        def centre(field):
            return field[:, LANE:LANE + CHUNK]

        through = None
        for p in range(CZ):
            def load(field):
                return fields[field * 32 + p * BAND:field * 32 + (p + 1) * BAND, window]

            ux = centre(smooth_x(load(3)))
            uy = smooth_x(load(4))
            uz = smooth_x(load(5))
            curl = centre(smooth_x(load(0)))
            square = curl * curl
            curl = centre(smooth_x(load(1)) - slope_x(uz))
            square += curl * curl
            curl = centre(slope_x(uy) - smooth_x(load(2)))
            density = (square + curl * curl) * scale
            left = jnp.exp(-density)
            tinted = [jnp.tanh(u) for u in (ux, centre(uy), centre(uz))]
            if through is None:
                weight = 1.0 - left
                through, depth = left, density
                sums = [weight * u for u in tinted]
            else:
                weight = through * (1.0 - left)
                through, depth = through * left, depth + density
                sums = [s + weight * u for s, u in zip(sums, tinted)]
        parts = sums + [depth]
        if not exchange:
            for q, part in enumerate(parts):
                out[q, :, pl.ds(c * CHUNK, CHUNK)] = part
            continue
        for q, part in enumerate(parts):
            for j in range(8):
                staged[:, q * 8 + j, :] = part[:, j * LANE:(j + 1) * LANE]
        outbox[pl.ds(c * BAND, BAND)] = staged[...].astype(jnp.bfloat16)

        def post(r, _):
            owner = r * (nx // CHUNK) + c

            @pl.when(owner != me)
            def _():
                pltpu.make_async_remote_copy(
                    src_ref=outbox.at[c * BAND + r], dst_ref=inbox.at[me], send_sem=out_s.at[owner],
                    recv_sem=in_r.at[me], device_id=(owner,), device_id_type=MESH).start()

            @pl.when(owner == me)
            def _():
                inbox[me] = outbox[c * BAND + r]

            return 0

        lax.fori_loop(0, BAND, post, 0)

    if exchange:
        def arrived(hop, _):
            source = lax.rem(me + hop, n)
            pltpu.make_async_remote_copy(
                src_ref=outbox.at[0], dst_ref=inbox.at[source], send_sem=out_s.at[source],
                recv_sem=in_r.at[source], device_id=(source,), device_id_type=MESH).wait_recv()
            return 0

        lax.fori_loop(1, n, arrived, 0)
        through = jnp.ones((8, LANE), jnp.float32)
        total = [jnp.zeros((8, LANE), jnp.float32) for _ in range(3)]
        for s in range(n):
            block = inbox[s].astype(jnp.float32)
            left = jnp.exp(-block[24:32])
            half = 0.5 * through
            cover = 1.0 - left
            total = [t + half * (cover + block[q * 8:q * 8 + 8]) for q, t in enumerate(total)]
            through = through * left
        total.append(1.0 - through)
        for q, value in enumerate(total):
            for j in range(8):
                out[q:q + 1, pl.ds(j * LANE, LANE)] = value[j:j + 1, :]

        def left_home(hop, _):
            other = lax.rem(me + hop, n)
            pltpu.make_async_remote_copy(
                src_ref=outbox.at[0], dst_ref=inbox.at[me], send_sem=out_s.at[other],
                recv_sem=in_r.at[me], device_id=(other,), device_id_type=MESH).wait_send()
            return 0

        lax.fori_loop(1, n, left_home, 0)
    for k in range(len(pieces)):
        for copy in halo_copies(k):
            copy.wait_send()


def per_device(velocity):
    n = lax.axis_size("slab")
    nx = velocity.shape[3]
    pixels = BAND * nx // n
    exchange = pixels == CHUNK
    pieces = sum(len(cut) for cut in spans(nx))
    bf16, f32 = jnp.bfloat16, jnp.float32
    scratch = [
        pltpu.VMEM((128, nx), bf16),
        pltpu.VMEM((2 * SIDE, nx), bf16),
        pltpu.VMEM((FIELDS * 32, nx + 2 * MARGIN), f32),
    ]
    if exchange:
        scratch += [
            pltpu.VMEM((BAND, 32, LANE), f32),
            pltpu.VMEM((n, 32, LANE), bf16),
            pltpu.VMEM((n, 32, LANE), bf16),
        ]
    scratch += [pltpu.SemaphoreType.DMA((pieces,))] * 4
    if exchange:
        scratch += [pltpu.SemaphoreType.DMA((n,))] * 2
    shape = (4, pixels) if exchange else (4, BAND, nx)
    result = pl.pallas_call(
        functools.partial(kernel, n, exchange, nx),
        out_shape=jax.ShapeDtypeStruct(shape, f32),
        in_specs=[pl.BlockSpec(memory_space=pltpu.VMEM)] * 2,
        out_specs=pl.BlockSpec(memory_space=pltpu.VMEM),
        scratch_shapes=scratch,
        compiler_params=pltpu.CompilerParams(
            collective_id=0, has_side_effects=True, vmem_limit_bytes=48 * 1024 * 1024
        ),
    )(velocity.reshape(3 * CZ * YH, nx), jnp.asarray(weights()))
    if exchange:
        return result
    parts = result.reshape(4, n, pixels).transpose(1, 0, 2).astype(bf16)
    parts = lax.all_to_all(parts, "slab", 0, 0, tiled=True).astype(f32)
    depth = parts[:, 3]
    before = jnp.exp(-(jnp.cumsum(depth, axis=0) - depth))
    cover = 1.0 - jnp.exp(-depth)
    colours = jnp.sum(0.5 * before[:, None] * (cover[:, None] + parts[:, :3]), axis=0)
    return jnp.concatenate([colours, (1.0 - jnp.exp(-jnp.sum(depth, axis=0)))[None]], axis=0)


def solution(mesh):
    return jax.shard_map(
        per_device, mesh=mesh, in_specs=(P(None, "slab", None, None),), out_specs=P(None, "slab"), check_vma=False
    )
```

```python
import functools

import jax
import jax.numpy as jnp
import ml_dtypes
import numpy as np
from jax import lax
from jax.experimental import pallas as pl
from jax.experimental.pallas import tpu as pltpu
from jax.sharding import PartitionSpec as P

MESH = pl.DeviceIdType.MESH
opacity_gain = 5.0

smooth_taps = np.array([1, 4, 6, 4, 1]) / 16.0
slope_taps = np.array([1, -8, 0, 8, -1]) / 1.0
both_taps = np.convolve(smooth_taps, slope_taps)
CZ, YH, BAND = 4, 16, 8
KEEP = YH - 4
FIELDS = 6
LANE = 128
SIDE = 96
CHUNK = 1024
TILE = 512
CELL = 256


def halo_row(component, plane, row):
    below = plane < 0
    source = plane + CZ if below else plane - CZ
    spec, band = (0, 32) if below else (SIDE + 64, SIDE)
    near = source - 2 if below else source
    if component < 2 and 2 <= row < 2 + BAND:
        return band + 32 * component + source * BAND + row - 2
    assert component != 1 and 0 <= near < 2
    if component == 0:
        return spec + near * 4 + (row if row < 2 else row - BAND)
    return spec + 8 + near * KEEP + row


def weights():
    send = np.zeros((128, 192))
    own = np.zeros((FIELDS * 32, 192))
    halo = np.zeros((FIELDS * 32, 192))

    def put(at, component, source, row):
        for b in range(5):
            send[at, component * 64 + source * YH + row + b] += smooth_taps[b]

    for component in range(2):
        for source in range(CZ):
            for r in range(BAND):
                put(32 + 32 * component + source * BAND + r, component, source, r + 2)
    for start, planes in ((0, (2, 3)), (96, (0, 1))):
        for near, source in enumerate(planes):
            for i, row in enumerate((0, 1, 10, 11)):
                put(start + near * 4 + i, 0, source, row)
            for row in range(KEEP):
                put(start + 8 + near * KEEP + row, 2, source, row)

    def term(field, component, z_taps, y_slope, sign):
        y_own = both_taps if y_slope else smooth_taps
        y_halo = slope_taps if y_slope else np.ones(1)
        for p in range(CZ):
            for r in range(BAND):
                at = field * 32 + p * BAND + r
                for a, wz in enumerate(z_taps):
                    plane = p + a - len(z_taps) // 2
                    if wz == 0:
                        continue
                    if 0 <= plane < CZ:
                        for b, wy in enumerate(y_own):
                            row = r + 4 + b - len(y_own) // 2
                            own[at, component * 64 + plane * YH + row] += sign * wz * wy / 16.0
                    else:
                        for b, wy in enumerate(y_halo):
                            if wy:
                                row = r + 2 + b - len(y_halo) // 2
                                halo[at, halo_row(component, plane, row)] += sign * wz * wy / 16.0

    term(0, 2, smooth_taps, True, 1.0)
    term(0, 1, both_taps, False, -1.0)
    term(1, 0, both_taps, False, 1.0)
    term(2, 0, smooth_taps, True, 1.0)
    for k in range(3):
        term(3 + k, k, smooth_taps, False, 1.0)
    full = np.concatenate([send, own, halo], axis=0)
    rounded = full.astype(ml_dtypes.bfloat16)
    assert np.all(rounded.astype(np.float64) == full)
    return rounded


def shift(field, by):
    return pltpu.roll(field, by % field.shape[1], 1)


def smooth_x(field):
    for _ in range(2):
        field = field + shift(field, 1)
        field = field + shift(field, -1)
    return field


def slope_x(field):
    near = shift(field, -1) - shift(field, 1)
    return 8.0 * near - (shift(near, 1) + shift(near, -1))


def kernel(n, exchange, nx, raw_hbm, mats, out, raw, send, halo, fields, *rest):
    if exchange:
        staged, outbox, inbox, in_s, up_s, up_r, down_s, down_r, out_s, in_r = rest
    else:
        in_s, up_s, up_r, down_s, down_r = rest
    me = lax.axis_index("slab")
    up, down = lax.rem(me + 1, n), lax.rem(me + n - 1, n)
    barrier = pltpu.get_barrier_semaphore()
    chunks, tiles, cells = nx // CHUNK, nx // TILE, nx // CELL

    inward = [
        pltpu.make_async_copy(raw_hbm.at[:, pl.ds(first, width)], raw.at[:, pl.ds(at, width)], in_s.at[i])
        for i, (first, width, at) in enumerate(((nx - LANE, LANE, 0), (0, LANE, nx + LANE), (0, nx, LANE)))
    ]
    for copy in inward:
        copy.start()
    if exchange:
        def greet(hop, _):
            pl.semaphore_signal(barrier, inc=1, device_id=(lax.rem(me + hop, n),), device_id_type=MESH)
            return 0

        lax.fori_loop(1, n, greet, 0)
    else:
        for other in (up, down):
            pl.semaphore_signal(barrier, inc=1, device_id=(other,), device_id_type=MESH)

    pieces = [(nx - CELL, CELL, 1, 0), (0, TILE, 2, 0), (TILE, CHUNK + CELL - TILE, 4, 0)]
    for c in range(1, chunks):
        first = c * CHUNK + CELL
        pieces.append((first, min(CHUNK, nx - CELL - first), min(4 + 2 * c, tiles), c))

    def halo_copies(k):
        first, width, _, _ = pieces[k]
        lanes = pl.ds(first, width)
        return (
            pltpu.make_async_remote_copy(
                src_ref=send.at[pl.ds(0, SIDE), lanes], dst_ref=halo.at[pl.ds(0, SIDE), lanes],
                send_sem=up_s.at[k], recv_sem=up_r.at[k], device_id=(up,), device_id_type=MESH),
            pltpu.make_async_remote_copy(
                src_ref=send.at[pl.ds(32, SIDE), lanes], dst_ref=halo.at[pl.ds(SIDE, SIDE), lanes],
                send_sem=down_s.at[k], recv_sem=down_r.at[k], device_id=(down,), device_id_type=MESH),
        )

    def filtered(rows, first):
        window = raw[:, pl.ds(first, TILE + 2 * LANE)]
        return smooth_x(jnp.dot(mats[rows, :], window, preferred_element_type=jnp.float32))[:, LANE:LANE + TILE]

    def to_send(k, _):
        first = pl.multiple_of(lax.rem(k + tiles - 1, tiles) * TILE, TILE)
        send[:, pl.ds(first, TILE)] = filtered(slice(0, 128), first).astype(jnp.bfloat16)
        for i, (_, _, ready, _) in enumerate(pieces):
            @pl.when(k == ready - 1)
            def _():
                for copy in halo_copies(i):
                    copy.start()
        return 0

    for copy in inward:
        copy.wait()
    pl.semaphore_wait(barrier, n - 1 if exchange else 2)
    lax.fori_loop(0, tiles, to_send, 0)

    def own(k, _):
        first = pl.multiple_of(k * TILE, TILE)
        fields[:, pl.ds(first + LANE, TILE)] = filtered(slice(128, 320), first)
        return 0

    lax.fori_loop(0, tiles, own, 0)

    def add_halo(k, _):
        first = pl.multiple_of(lax.rem(k + cells - 1, cells) * CELL, CELL)
        more = jnp.dot(mats[320:512, :], halo[:, pl.ds(first, CELL)], preferred_element_type=jnp.float32)
        total = fields[:, pl.ds(first + LANE, CELL)] + more
        fields[:, pl.ds(first + LANE, CELL)] = total

        @pl.when(first == 0)
        def _():
            fields[128:192, nx + LANE:nx + 2 * LANE] = total[128:192, 0:LANE]

        @pl.when(first == nx - CELL)
        def _():
            fields[128:192, 0:LANE] = total[128:192, CELL - LANE:CELL]

        return 0

    scale = opacity_gain / (144.0 * CZ * n)
    per_chunk = CHUNK // CELL

    def shade(k, _):
        first = pl.multiple_of(k * CELL, CELL)
        through = None
        for p in range(CZ):
            def centre(field):
                return fields[field * 32 + p * BAND:field * 32 + (p + 1) * BAND, pl.ds(first + LANE, CELL)]

            def slope(field):
                window = fields[field * 32 + p * BAND:field * 32 + (p + 1) * BAND, pl.ds(first, CELL + 2 * LANE)]
                return slope_x(window)[:, LANE:LANE + CELL]

            curl = centre(0)
            square = curl * curl
            curl = centre(1) - slope(5)
            square += curl * curl
            curl = slope(4) - centre(2)
            density = (square + curl * curl) * scale
            left = jnp.exp(-density)
            tinted = [jnp.tanh(centre(3 + q)) for q in range(3)]
            if through is None:
                weight = 1.0 - left
                through, depth = left, density
                sums = [weight * u for u in tinted]
            else:
                weight = through * (1.0 - left)
                through, depth = through * left, depth + density
                sums = [s + weight * u for s, u in zip(sums, tinted)]
        for q, part in enumerate(sums + [depth]):
            if not exchange:
                out[q, :, pl.ds(first, CELL)] = part
                continue
            for j in range(CELL // LANE):
                row = q * 8 + lax.rem(k, per_chunk) * (CELL // LANE) + j
                staged[pl.ds(pl.multiple_of(row * BAND, BAND), BAND), :] = part[:, j * LANE:(j + 1) * LANE]
        return 0

    def one_chunk(c, _):
        for i, (_, _, _, chunk) in enumerate(pieces):
            @pl.when(c == chunk)
            def _():
                for copy in halo_copies(i):
                    copy.wait_recv()

        begin = jnp.where(c == 0, 0, c * per_chunk + 2)
        lax.fori_loop(begin, jnp.minimum((c + 1) * per_chunk + 2, cells), add_halo, 0)
        lax.fori_loop(c * per_chunk, (c + 1) * per_chunk, shade, 0)
        if not exchange:
            return 0
        for r in range(BAND):
            outbox[c * BAND + r] = staged[pl.ds(r, 32, stride=BAND), :].astype(jnp.bfloat16)

        def post(r, _):
            owner = r * chunks + c

            @pl.when(owner != me)
            def _():
                pltpu.make_async_remote_copy(
                    src_ref=outbox.at[c * BAND + r], dst_ref=inbox.at[me], send_sem=out_s.at[owner],
                    recv_sem=in_r.at[me], device_id=(owner,), device_id_type=MESH).start()

            @pl.when(owner == me)
            def _():
                inbox[me] = outbox[c * BAND + r]

            return 0

        lax.fori_loop(0, BAND, post, 0)
        return 0

    lax.fori_loop(0, chunks, one_chunk, 0)

    if exchange:
        def arrived(hop, _):
            source = lax.rem(me + hop, n)
            pltpu.make_async_remote_copy(
                src_ref=outbox.at[0], dst_ref=inbox.at[source], send_sem=out_s.at[source],
                recv_sem=in_r.at[source], device_id=(source,), device_id_type=MESH).wait_recv()
            return 0

        lax.fori_loop(1, n, arrived, 0)
        through = jnp.ones((8, LANE), jnp.float32)
        total = [jnp.zeros((8, LANE), jnp.float32) for _ in range(3)]
        for s in range(n):
            block = inbox[s].astype(jnp.float32)
            left = jnp.exp(-block[24:32])
            half = 0.5 * through
            cover = 1.0 - left
            total = [t + half * (cover + block[q * 8:q * 8 + 8]) for q, t in enumerate(total)]
            through = through * left
        total.append(1.0 - through)
        for q, value in enumerate(total):
            for j in range(8):
                out[q:q + 1, pl.ds(j * LANE, LANE)] = value[j:j + 1, :]

        def left_home(hop, _):
            other = lax.rem(me + hop, n)
            pltpu.make_async_remote_copy(
                src_ref=outbox.at[0], dst_ref=inbox.at[me], send_sem=out_s.at[other],
                recv_sem=in_r.at[me], device_id=(other,), device_id_type=MESH).wait_send()
            return 0

        lax.fori_loop(1, n, left_home, 0)
    for k in range(len(pieces)):
        for copy in halo_copies(k):
            copy.wait_send()


def per_device(velocity):
    n = lax.axis_size("slab")
    nx = velocity.shape[3]
    pixels = BAND * nx // n
    exchange = pixels == CHUNK
    pieces = 2 + nx // CHUNK
    bf16, f32 = jnp.bfloat16, jnp.float32
    scratch = [
        pltpu.VMEM((192, nx + 2 * LANE), bf16),
        pltpu.VMEM((128, nx), bf16),
        pltpu.VMEM((2 * SIDE, nx), bf16),
        pltpu.VMEM((FIELDS * 32, nx + 2 * LANE), f32),
    ]
    if exchange:
        scratch += [
            pltpu.VMEM((32 * BAND, LANE), f32),
            pltpu.VMEM((n, 32, LANE), bf16),
            pltpu.VMEM((n, 32, LANE), bf16),
        ]
    scratch += [pltpu.SemaphoreType.DMA((3,))]
    scratch += [pltpu.SemaphoreType.DMA((pieces,))] * 4
    if exchange:
        scratch += [pltpu.SemaphoreType.DMA((n,))] * 2
    shape = (4, pixels) if exchange else (4, BAND, nx)
    result = pl.pallas_call(
        functools.partial(kernel, n, exchange, nx),
        out_shape=jax.ShapeDtypeStruct(shape, f32),
        in_specs=[pl.BlockSpec(memory_space=pl.ANY), pl.BlockSpec(memory_space=pltpu.VMEM)],
        out_specs=pl.BlockSpec(memory_space=pltpu.VMEM),
        scratch_shapes=scratch,
        compiler_params=pltpu.CompilerParams(
            collective_id=0, has_side_effects=True, vmem_limit_bytes=48 * 1024 * 1024
        ),
    )(velocity.reshape(3 * CZ * YH, nx), jnp.asarray(weights()))
    if exchange:
        return result
    parts = result.reshape(4, n, pixels).transpose(1, 0, 2).astype(bf16)
    parts = lax.all_to_all(parts, "slab", 0, 0, tiled=True).astype(f32)
    depth = parts[:, 3]
    before = jnp.exp(-(jnp.cumsum(depth, axis=0) - depth))
    cover = 1.0 - jnp.exp(-depth)
    colours = jnp.sum(0.5 * before[:, None] * (cover[:, None] + parts[:, :3]), axis=0)
    return jnp.concatenate([colours, (1.0 - jnp.exp(-jnp.sum(depth, axis=0)))[None]], axis=0)


def solution(mesh):
    return jax.shard_map(
        per_device, mesh=mesh, in_specs=(P(None, "slab", None, None),), out_specs=P(None, "slab"), check_vma=False
    )
```

```python
import functools

import jax
import jax.numpy as jnp
import ml_dtypes
import numpy as np
from jax import lax
from jax.experimental import pallas as pl
from jax.experimental.pallas import tpu as pltpu
from jax.sharding import PartitionSpec as P

MESH = pl.DeviceIdType.MESH
opacity_gain = 5.0

smooth_taps = np.array([1, 4, 6, 4, 1]) / 16.0
slope_taps = np.array([1, -8, 0, 8, -1]) / 1.0
both_taps = np.convolve(smooth_taps, slope_taps)
CZ, YH, BAND = 4, 16, 8
KEEP = YH - 4
FIELDS = 6
LANE = 128
SIDE = 96
CHUNK = 1024
TILE = 512
CELL = 256
FLIGHT = 4


def halo_row(component, plane, row):
    below = plane < 0
    source = plane + CZ if below else plane - CZ
    spec, band = (0, 32) if below else (SIDE + 64, SIDE)
    near = source - 2 if below else source
    if component < 2 and 2 <= row < 2 + BAND:
        return band + 32 * component + source * BAND + row - 2
    assert component != 1 and 0 <= near < 2
    if component == 0:
        return spec + near * 4 + (row if row < 2 else row - BAND)
    return spec + 8 + near * KEEP + row


def weights():
    send = np.zeros((128, 192))
    own = np.zeros((FIELDS * 32, 192))
    halo = np.zeros((FIELDS * 32, 192))

    def put(at, component, source, row):
        for b in range(5):
            send[at, component * 64 + source * YH + row + b] += smooth_taps[b]

    for component in range(2):
        for source in range(CZ):
            for r in range(BAND):
                put(32 + 32 * component + source * BAND + r, component, source, r + 2)
    for start, planes in ((0, (2, 3)), (96, (0, 1))):
        for near, source in enumerate(planes):
            for i, row in enumerate((0, 1, 10, 11)):
                put(start + near * 4 + i, 0, source, row)
            for row in range(KEEP):
                put(start + 8 + near * KEEP + row, 2, source, row)

    def term(field, component, z_taps, y_slope, sign):
        y_own = both_taps if y_slope else smooth_taps
        y_halo = slope_taps if y_slope else np.ones(1)
        for p in range(CZ):
            for r in range(BAND):
                at = field * 32 + p * BAND + r
                for a, wz in enumerate(z_taps):
                    plane = p + a - len(z_taps) // 2
                    if wz == 0:
                        continue
                    if 0 <= plane < CZ:
                        for b, wy in enumerate(y_own):
                            row = r + 4 + b - len(y_own) // 2
                            own[at, component * 64 + plane * YH + row] += sign * wz * wy / 16.0
                    else:
                        for b, wy in enumerate(y_halo):
                            if wy:
                                row = r + 2 + b - len(y_halo) // 2
                                halo[at, halo_row(component, plane, row)] += sign * wz * wy / 16.0

    term(0, 2, smooth_taps, True, 1.0)
    term(0, 1, both_taps, False, -1.0)
    term(1, 0, both_taps, False, 1.0)
    term(2, 0, smooth_taps, True, 1.0)
    for k in range(3):
        term(3 + k, k, smooth_taps, False, 1.0)
    full = np.concatenate([send, own, halo], axis=0)
    rounded = full.astype(ml_dtypes.bfloat16)
    assert np.all(rounded.astype(np.float64) == full)
    return rounded


def shift(field, by):
    return pltpu.roll(field, by % field.shape[1], 1)


def smooth_x(field):
    for _ in range(2):
        field = field + shift(field, 1)
        field = field + shift(field, -1)
    return field


def slope_x(field):
    near = shift(field, -1) - shift(field, 1)
    return 8.0 * near - (shift(near, 1) + shift(near, -1))


def kernel(n, exchange, nx, raw_hbm, mats_hbm, out, raw, mats, send, halo, fields, *rest):
    if exchange:
        staged, outbox, inbox, in_s, up_s, up_r, down_s, down_r, out_s, in_r = rest
    else:
        in_s, up_s, up_r, down_s, down_r = rest
    me = lax.axis_index("slab")
    up, down = lax.rem(me + 1, n), lax.rem(me + n - 1, n)
    barrier = pltpu.get_barrier_semaphore()
    chunks, tiles, cells = nx // CHUNK, nx // TILE, nx // CELL

    inward = [pltpu.make_async_copy(mats_hbm, mats, in_s.at[0])]
    for i, (first, width, at) in enumerate((
        (nx - CELL - LANE, LANE + CELL, 0),
        (0, CHUNK, LANE + CELL),
        (CHUNK, nx - CELL - CHUNK, LANE + CELL + CHUNK),
        (nx - CELL, LANE, LANE + nx),
    )):
        inward.append(pltpu.make_async_copy(
            raw_hbm.at[:, pl.ds(first, width)], raw.at[:, pl.ds(at, width)], in_s.at[i + 1]))
    for copy in inward:
        copy.start()
    if exchange:
        def greet(hop, _):
            pl.semaphore_signal(barrier, inc=1, device_id=(lax.rem(me + hop, n),), device_id_type=MESH)
            return 0

        lax.fori_loop(1, n, greet, 0)
    else:
        for other in (up, down):
            pl.semaphore_signal(barrier, inc=1, device_id=(other,), device_id_type=MESH)

    def halo_copies(k):
        lanes = pl.ds(pl.multiple_of(k * TILE, TILE), TILE)
        return (
            pltpu.make_async_remote_copy(
                src_ref=send.at[pl.ds(0, SIDE), lanes], dst_ref=halo.at[pl.ds(0, SIDE), lanes],
                send_sem=up_s.at[k], recv_sem=up_r.at[k], device_id=(up,), device_id_type=MESH),
            pltpu.make_async_remote_copy(
                src_ref=send.at[pl.ds(32, SIDE), lanes], dst_ref=halo.at[pl.ds(SIDE, SIDE), lanes],
                send_sem=down_s.at[k], recv_sem=down_r.at[k], device_id=(down,), device_id_type=MESH),
        )

    def filtered(rows, first):
        window = raw[:, pl.ds(first, TILE + 2 * LANE)]
        return smooth_x(jnp.dot(mats[rows, :], window, preferred_element_type=jnp.float32))[:, LANE:LANE + TILE]

    def to_send(k, _):
        first = pl.multiple_of(k * TILE, TILE)

        @pl.when(k == 2)
        def _():
            for copy in inward[3:]:
                copy.wait()

        send[:, pl.ds(first, TILE)] = filtered(slice(0, 128), first).astype(jnp.bfloat16)

        @pl.when(k == 0)
        def _():
            pl.semaphore_wait(barrier, n - 1 if exchange else 2)

        @pl.when(k < FLIGHT)
        def _():
            for copy in halo_copies(k):
                copy.start()

        return 0

    for copy in inward[:3]:
        copy.wait()
    lax.fori_loop(0, tiles, to_send, 0)

    def own(k, _):
        first = pl.multiple_of(k * TILE, TILE)
        fields[:, pl.ds(first + LANE, TILE)] = filtered(slice(128, 320), first)

        @pl.when(k + FLIGHT < tiles)
        def _():
            for copy in halo_copies(k):
                copy.wait_send()
            for copy in halo_copies(k + FLIGHT):
                copy.start()

        return 0

    lax.fori_loop(0, tiles, own, 0)

    def add_halo(k, _):
        first = pl.multiple_of(k * CELL, CELL)
        more = jnp.dot(mats[320:512, :], halo[:, pl.ds(first, CELL)], preferred_element_type=jnp.float32)
        total = fields[:, pl.ds(first + LANE, CELL)] + more
        fields[:, pl.ds(first + LANE, CELL)] = total

        @pl.when(first == 0)
        def _():
            fields[128:192, nx + LANE:nx + 2 * LANE] = total[128:192, 0:LANE]

        @pl.when(first == nx - CELL)
        def _():
            fields[128:192, 0:LANE] = total[128:192, CELL - LANE:CELL]

        return 0

    scale = opacity_gain / (144.0 * CZ * n)
    per_chunk = CHUNK // CELL

    def shade(k, _):
        first = pl.multiple_of(lax.rem(k + 1, cells) * CELL, CELL)
        through = None
        for p in range(CZ):
            def centre(field):
                return fields[field * 32 + p * BAND:field * 32 + (p + 1) * BAND, pl.ds(first + LANE, CELL)]

            def slope(field):
                window = fields[field * 32 + p * BAND:field * 32 + (p + 1) * BAND, pl.ds(first, CELL + 2 * LANE)]
                return slope_x(window)[:, LANE:LANE + CELL]

            curl = centre(0)
            square = curl * curl
            curl = centre(1) - slope(5)
            square += curl * curl
            curl = slope(4) - centre(2)
            density = (square + curl * curl) * scale
            left = jnp.exp(-density)
            tinted = [jnp.tanh(centre(3 + q)) for q in range(3)]
            if through is None:
                weight = 1.0 - left
                through, depth = left, density
                sums = [weight * u for u in tinted]
            else:
                weight = through * (1.0 - left)
                through, depth = through * left, depth + density
                sums = [s + weight * u for s, u in zip(sums, tinted)]
        for q, part in enumerate(sums + [depth]):
            if not exchange:
                out[q, :, pl.ds(pl.multiple_of(k * CELL, CELL), CELL)] = part
                continue
            for j in range(CELL // LANE):
                row = q * 8 + lax.rem(k, per_chunk) * (CELL // LANE) + j
                staged[pl.ds(pl.multiple_of(row * BAND, BAND), BAND), :] = part[:, j * LANE:(j + 1) * LANE]
        return 0

    per_tile = TILE // CELL

    def one_tile(k, _):
        for copy in halo_copies(k):
            copy.wait_recv()
        lax.fori_loop(k * per_tile, (k + 1) * per_tile, add_halo, 0)
        return 0

    def one_chunk(c, _):
        ready = CHUNK // TILE
        lax.fori_loop(jnp.where(c == 0, 0, c * ready + 1), jnp.minimum((c + 1) * ready + 1, tiles), one_tile, 0)
        lax.fori_loop(c * per_chunk, (c + 1) * per_chunk, shade, 0)
        if not exchange:
            return 0
        for r in range(BAND):
            outbox[c * BAND + r] = staged[pl.ds(r, 32, stride=BAND), :].astype(jnp.bfloat16)

        def post(r, _):
            owner = r * chunks + c

            @pl.when(owner != me)
            def _():
                pltpu.make_async_remote_copy(
                    src_ref=outbox.at[c * BAND + r], dst_ref=inbox.at[me], send_sem=out_s.at[owner],
                    recv_sem=in_r.at[me], device_id=(owner,), device_id_type=MESH).start()

            @pl.when(owner == me)
            def _():
                inbox[me] = outbox[c * BAND + r]

            return 0

        lax.fori_loop(0, BAND, post, 0)
        return 0

    lax.fori_loop(0, chunks, one_chunk, 0)

    if exchange:
        def arrived(hop, _):
            source = lax.rem(me + hop, n)
            pltpu.make_async_remote_copy(
                src_ref=outbox.at[0], dst_ref=inbox.at[source], send_sem=out_s.at[source],
                recv_sem=in_r.at[source], device_id=(source,), device_id_type=MESH).wait_recv()
            return 0

        lax.fori_loop(1, n, arrived, 0)
        through = jnp.ones((8, LANE), jnp.float32)
        total = [jnp.zeros((8, LANE), jnp.float32) for _ in range(3)]
        for s in range(n):
            block = inbox[s].astype(jnp.float32)
            left = jnp.exp(-block[24:32])
            half = 0.5 * through
            cover = 1.0 - left
            total = [t + half * (cover + block[q * 8:q * 8 + 8]) for q, t in enumerate(total)]
            through = through * left
        total.append(1.0 - through)
        for q, value in enumerate(total):
            for j in range(8):
                out[q:q + 1, pl.ds(j * LANE, LANE)] = value[j:j + 1, :]

        def left_home(hop, _):
            other = lax.rem(me + hop, n)
            pltpu.make_async_remote_copy(
                src_ref=outbox.at[0], dst_ref=inbox.at[me], send_sem=out_s.at[other],
                recv_sem=in_r.at[me], device_id=(other,), device_id_type=MESH).wait_send()
            return 0

        lax.fori_loop(1, n, left_home, 0)
    for k in range(tiles - FLIGHT, tiles):
        for copy in halo_copies(k):
            copy.wait_send()


def per_device(velocity):
    n = lax.axis_size("slab")
    nx = velocity.shape[3]
    pixels = BAND * nx // n
    exchange = pixels == CHUNK
    tiles = nx // TILE
    bf16, f32 = jnp.bfloat16, jnp.float32
    scratch = [
        pltpu.VMEM((192, nx + 2 * LANE), bf16),
        pltpu.VMEM((512, 192), bf16),
        pltpu.VMEM((128, nx), bf16),
        pltpu.VMEM((2 * SIDE, nx), bf16),
        pltpu.VMEM((FIELDS * 32, nx + 2 * LANE), f32),
    ]
    if exchange:
        scratch += [
            pltpu.VMEM((32 * BAND, LANE), f32),
            pltpu.VMEM((n, 32, LANE), bf16),
            pltpu.VMEM((n, 32, LANE), bf16),
        ]
    scratch += [pltpu.SemaphoreType.DMA((5,))]
    scratch += [pltpu.SemaphoreType.DMA((tiles,))] * 4
    if exchange:
        scratch += [pltpu.SemaphoreType.DMA((n,))] * 2
    shape = (4, pixels) if exchange else (4, BAND, nx)
    result = pl.pallas_call(
        functools.partial(kernel, n, exchange, nx),
        out_shape=jax.ShapeDtypeStruct(shape, f32),
        in_specs=[pl.BlockSpec(memory_space=pl.ANY)] * 2,
        out_specs=pl.BlockSpec(memory_space=pltpu.VMEM),
        scratch_shapes=scratch,
        compiler_params=pltpu.CompilerParams(
            collective_id=0, has_side_effects=True, vmem_limit_bytes=60 * 1024 * 1024
        ),
    )(velocity.reshape(3 * CZ * YH, nx), jnp.asarray(weights()))
    if exchange:
        return result
    parts = result.reshape(4, n, pixels).transpose(1, 0, 2).astype(bf16)
    parts = lax.all_to_all(parts, "slab", 0, 0, tiled=True).astype(f32)
    depth = parts[:, 3]
    before = jnp.exp(-(jnp.cumsum(depth, axis=0) - depth))
    cover = 1.0 - jnp.exp(-depth)
    colours = jnp.sum(0.5 * before[:, None] * (cover[:, None] + parts[:, :3]), axis=0)
    return jnp.concatenate([colours, (1.0 - jnp.exp(-jnp.sum(depth, axis=0)))[None]], axis=0)


def solution(mesh):
    return jax.shard_map(
        per_device, mesh=mesh, in_specs=(P(None, "slab", None, None),), out_specs=P(None, "slab"), check_vma=False
    )
```

```python
import functools

import jax
import jax.numpy as jnp
import ml_dtypes
import numpy as np
from jax import lax
from jax.experimental import pallas as pl
from jax.experimental.pallas import tpu as pltpu
from jax.sharding import PartitionSpec as P

MESH = pl.DeviceIdType.MESH
opacity_gain = 5.0

smooth_taps = np.array([1, 4, 6, 4, 1]) / 16.0
slope_taps = np.array([1, -8, 0, 8, -1]) / 1.0
both_taps = np.convolve(smooth_taps, slope_taps)
CZ, YH, BAND = 4, 16, 8
KEEP = YH - 4
FIELDS = 6
LANE = 128
SIDE = 96
CHUNK = 1024
TILE = 512
CELL = 256
FLIGHT = 4


def halo_row(component, plane, row):
    below = plane < 0
    source = plane + CZ if below else plane - CZ
    spec, band = (0, 32) if below else (SIDE + 64, SIDE)
    near = source - 2 if below else source
    if component < 2 and 2 <= row < 2 + BAND:
        return band + 32 * component + source * BAND + row - 2
    assert component != 1 and 0 <= near < 2
    if component == 0:
        return spec + near * 4 + (row if row < 2 else row - BAND)
    return spec + 8 + near * KEEP + row


def weights():
    send = np.zeros((128, 192))
    own = np.zeros((FIELDS * 32, 192))
    halo = np.zeros((FIELDS * 32, 192))

    def put(at, component, source, row):
        for b in range(5):
            send[at, component * 64 + source * YH + row + b] += smooth_taps[b]

    for component in range(2):
        for source in range(CZ):
            for r in range(BAND):
                put(32 + 32 * component + source * BAND + r, component, source, r + 2)
    for start, planes in ((0, (2, 3)), (96, (0, 1))):
        for near, source in enumerate(planes):
            for i, row in enumerate((0, 1, 10, 11)):
                put(start + near * 4 + i, 0, source, row)
            for row in range(KEEP):
                put(start + 8 + near * KEEP + row, 2, source, row)

    def term(field, component, z_taps, y_slope, sign):
        y_own = both_taps if y_slope else smooth_taps
        y_halo = slope_taps if y_slope else np.ones(1)
        for p in range(CZ):
            for r in range(BAND):
                at = field * 32 + p * BAND + r
                for a, wz in enumerate(z_taps):
                    plane = p + a - len(z_taps) // 2
                    if wz == 0:
                        continue
                    if 0 <= plane < CZ:
                        for b, wy in enumerate(y_own):
                            row = r + 4 + b - len(y_own) // 2
                            own[at, component * 64 + plane * YH + row] += sign * wz * wy / 16.0
                    else:
                        for b, wy in enumerate(y_halo):
                            if wy:
                                row = r + 2 + b - len(y_halo) // 2
                                halo[at, halo_row(component, plane, row)] += sign * wz * wy / 16.0

    term(0, 2, smooth_taps, True, 1.0)
    term(0, 1, both_taps, False, -1.0)
    term(1, 0, both_taps, False, 1.0)
    term(2, 0, smooth_taps, True, 1.0)
    for k in range(3):
        term(3 + k, k, smooth_taps, False, 1.0)
    full = np.concatenate([send, own, halo], axis=0)
    rounded = full.astype(ml_dtypes.bfloat16)
    assert np.all(rounded.astype(np.float64) == full)
    return rounded


def band(taps):
    matrix = np.zeros((CELL + 2 * LANE, CELL))
    for j in range(CELL):
        for o, tap in enumerate(taps):
            matrix[LANE + j + o - 2, j] = tap
    return matrix


def constants():
    zy = np.pad(weights(), ((0, 0), (0, CELL - 192)))
    along_x = np.concatenate([band(16.0 * smooth_taps), band(slope_taps)], axis=0)
    return np.concatenate([zy, along_x.astype(ml_dtypes.bfloat16)], axis=0)


def halves(field):
    high = field.astype(jnp.bfloat16)
    return high, (field - high.astype(jnp.float32)).astype(jnp.bfloat16)


def dot(a, b):
    return jnp.dot(a, b, preferred_element_type=jnp.float32)


def kernel(n, exchange, nx, raw_hbm, mats_hbm, out, raw, mats, high, low, send, halo, fields, *rest):
    if exchange:
        staged, outbox, inbox, in_s, up_s, up_r, down_s, down_r, out_s, in_r = rest
    else:
        in_s, up_s, up_r, down_s, down_r = rest
    me = lax.axis_index("slab")
    up, down = lax.rem(me + 1, n), lax.rem(me + n - 1, n)
    barrier = pltpu.get_barrier_semaphore()
    chunks, tiles, cells = nx // CHUNK, nx // TILE, nx // CELL

    inward = [pltpu.make_async_copy(mats_hbm, mats, in_s.at[0])]
    for i, (first, width, at) in enumerate((
        (nx - CELL - LANE, LANE + CELL, 0),
        (0, CHUNK, LANE + CELL),
        (CHUNK, nx - CELL - CHUNK, LANE + CELL + CHUNK),
        (nx - CELL, LANE, LANE + nx),
    )):
        inward.append(pltpu.make_async_copy(
            raw_hbm.at[:, pl.ds(first, width)], raw.at[:, pl.ds(at, width)], in_s.at[i + 1]))
    for copy in inward:
        copy.start()
    if exchange:
        def greet(hop, _):
            pl.semaphore_signal(barrier, inc=1, device_id=(lax.rem(me + hop, n),), device_id_type=MESH)
            return 0

        lax.fori_loop(1, n, greet, 0)
    else:
        for other in (up, down):
            pl.semaphore_signal(barrier, inc=1, device_id=(other,), device_id_type=MESH)

    def halo_copies(k):
        lanes = pl.ds(pl.multiple_of(k * TILE, TILE), TILE)
        return (
            pltpu.make_async_remote_copy(
                src_ref=send.at[pl.ds(0, SIDE), lanes], dst_ref=halo.at[pl.ds(0, SIDE), lanes],
                send_sem=up_s.at[k], recv_sem=up_r.at[k], device_id=(up,), device_id_type=MESH),
            pltpu.make_async_remote_copy(
                src_ref=send.at[pl.ds(32, SIDE), lanes], dst_ref=halo.at[pl.ds(SIDE, SIDE), lanes],
                send_sem=down_s.at[k], recv_sem=down_r.at[k], device_id=(down,), device_id_type=MESH),
        )

    def filtered(rows, lanes):
        matrix = mats[rows, 0:192]
        return dot(matrix, high[:, lanes]) + dot(matrix, low[:, lanes])

    def to_send(k, _):
        first = pl.multiple_of(k * TILE, TILE)

        @pl.when(k == 2)
        def _():
            for copy in inward[3:]:
                copy.wait()

        for cell in range(TILE // CELL):
            at = pl.multiple_of(first + cell * CELL, CELL)
            lanes = pl.ds(at, CELL)
            high[:, lanes], low[:, lanes] = halves(dot(raw[:, pl.ds(at, CELL + 2 * LANE)], mats[512:1024, :]))
        lanes = pl.ds(first, TILE)
        send[:, lanes] = filtered(slice(0, 128), lanes).astype(jnp.bfloat16)

        @pl.when(k == 0)
        def _():
            pl.semaphore_wait(barrier, n - 1 if exchange else 2)

        @pl.when(k < FLIGHT)
        def _():
            for copy in halo_copies(k):
                copy.start()

        return 0

    for copy in inward[:3]:
        copy.wait()
    lax.fori_loop(0, tiles, to_send, 0)

    def own(k, _):
        first = pl.multiple_of(k * TILE, TILE)
        fields[:, pl.ds(first + LANE, TILE)] = filtered(slice(128, 320), pl.ds(first, TILE))

        @pl.when(k + FLIGHT < tiles)
        def _():
            for copy in halo_copies(k):
                copy.wait_send()
            for copy in halo_copies(k + FLIGHT):
                copy.start()

        return 0

    lax.fori_loop(0, tiles, own, 0)

    def add_halo(k, _):
        first = pl.multiple_of(k * CELL, CELL)
        more = dot(mats[320:512, 0:192], halo[:, pl.ds(first, CELL)])
        total = fields[:, pl.ds(first + LANE, CELL)] + more
        fields[:, pl.ds(first + LANE, CELL)] = total

        @pl.when(first == 0)
        def _():
            fields[128:192, nx + LANE:nx + 2 * LANE] = total[128:192, 0:LANE]

        @pl.when(first == nx - CELL)
        def _():
            fields[128:192, 0:LANE] = total[128:192, CELL - LANE:CELL]

        return 0

    scale = opacity_gain / (144.0 * CZ * n)
    per_chunk = CHUNK // CELL

    def shade(k, _):
        first = pl.multiple_of(lax.rem(k + 1, cells) * CELL, CELL)
        slopes = sum(dot(half, mats[1024:1536, :]) for half in halves(fields[128:192, pl.ds(first, CELL + 2 * LANE)]))
        through = None
        for p in range(CZ):
            def centre(field):
                return fields[field * 32 + p * BAND:field * 32 + (p + 1) * BAND, pl.ds(first + LANE, CELL)]

            def slope(field):
                return slopes[(field - 4) * 32 + p * BAND:(field - 4) * 32 + (p + 1) * BAND]

            curl = centre(0)
            square = curl * curl
            curl = centre(1) - slope(5)
            square += curl * curl
            curl = slope(4) - centre(2)
            density = (square + curl * curl) * scale
            left = jnp.exp(-density)
            tinted = [jnp.tanh(centre(3 + q)) for q in range(3)]
            if through is None:
                weight = 1.0 - left
                through, depth = left, density
                sums = [weight * u for u in tinted]
            else:
                weight = through * (1.0 - left)
                through, depth = through * left, depth + density
                sums = [s + weight * u for s, u in zip(sums, tinted)]
        for q, part in enumerate(sums + [depth]):
            if not exchange:
                out[q, :, pl.ds(pl.multiple_of(k * CELL, CELL), CELL)] = part
                continue
            for j in range(CELL // LANE):
                row = q * 8 + lax.rem(k, per_chunk) * (CELL // LANE) + j
                staged[pl.ds(pl.multiple_of(row * BAND, BAND), BAND), :] = part[:, j * LANE:(j + 1) * LANE]
        return 0

    per_tile = TILE // CELL

    def one_tile(k, _):
        for copy in halo_copies(k):
            copy.wait_recv()
        lax.fori_loop(k * per_tile, (k + 1) * per_tile, add_halo, 0)
        return 0

    def one_chunk(c, _):
        ready = CHUNK // TILE
        lax.fori_loop(jnp.where(c == 0, 0, c * ready + 1), jnp.minimum((c + 1) * ready + 1, tiles), one_tile, 0)
        lax.fori_loop(c * per_chunk, (c + 1) * per_chunk, shade, 0)
        if not exchange:
            return 0
        for r in range(BAND):
            outbox[c * BAND + r] = staged[pl.ds(r, 32, stride=BAND), :].astype(jnp.bfloat16)

        def post(r, _):
            owner = r * chunks + c

            @pl.when(owner != me)
            def _():
                pltpu.make_async_remote_copy(
                    src_ref=outbox.at[c * BAND + r], dst_ref=inbox.at[me], send_sem=out_s.at[owner],
                    recv_sem=in_r.at[me], device_id=(owner,), device_id_type=MESH).start()

            @pl.when(owner == me)
            def _():
                inbox[me] = outbox[c * BAND + r]

            return 0

        lax.fori_loop(0, BAND, post, 0)
        return 0

    lax.fori_loop(0, chunks, one_chunk, 0)

    if exchange:
        def arrived(hop, _):
            source = lax.rem(me + hop, n)
            pltpu.make_async_remote_copy(
                src_ref=outbox.at[0], dst_ref=inbox.at[source], send_sem=out_s.at[source],
                recv_sem=in_r.at[source], device_id=(source,), device_id_type=MESH).wait_recv()
            return 0

        lax.fori_loop(1, n, arrived, 0)
        through = jnp.ones((8, LANE), jnp.float32)
        total = [jnp.zeros((8, LANE), jnp.float32) for _ in range(3)]
        for s in range(n):
            block = inbox[s].astype(jnp.float32)
            left = jnp.exp(-block[24:32])
            half = 0.5 * through
            cover = 1.0 - left
            total = [t + half * (cover + block[q * 8:q * 8 + 8]) for q, t in enumerate(total)]
            through = through * left
        total.append(1.0 - through)
        for q, value in enumerate(total):
            for j in range(8):
                out[q:q + 1, pl.ds(j * LANE, LANE)] = value[j:j + 1, :]

        def left_home(hop, _):
            other = lax.rem(me + hop, n)
            pltpu.make_async_remote_copy(
                src_ref=outbox.at[0], dst_ref=inbox.at[me], send_sem=out_s.at[other],
                recv_sem=in_r.at[me], device_id=(other,), device_id_type=MESH).wait_send()
            return 0

        lax.fori_loop(1, n, left_home, 0)
    for k in range(tiles - FLIGHT, tiles):
        for copy in halo_copies(k):
            copy.wait_send()


def per_device(velocity):
    n = lax.axis_size("slab")
    nx = velocity.shape[3]
    pixels = BAND * nx // n
    exchange = pixels == CHUNK
    tiles = nx // TILE
    bf16, f32 = jnp.bfloat16, jnp.float32
    scratch = [
        pltpu.VMEM((192, nx + 2 * LANE), bf16),
        pltpu.VMEM((512 + 2 * (CELL + 2 * LANE), CELL), bf16),
        pltpu.VMEM((192, nx), bf16),
        pltpu.VMEM((192, nx), bf16),
        pltpu.VMEM((128, nx), bf16),
        pltpu.VMEM((2 * SIDE, nx), bf16),
        pltpu.VMEM((FIELDS * 32, nx + 2 * LANE), f32),
    ]
    if exchange:
        scratch += [
            pltpu.VMEM((32 * BAND, LANE), f32),
            pltpu.VMEM((n, 32, LANE), bf16),
            pltpu.VMEM((n, 32, LANE), bf16),
        ]
    scratch += [pltpu.SemaphoreType.DMA((5,))]
    scratch += [pltpu.SemaphoreType.DMA((tiles,))] * 4
    if exchange:
        scratch += [pltpu.SemaphoreType.DMA((n,))] * 2
    shape = (4, pixels) if exchange else (4, BAND, nx)
    result = pl.pallas_call(
        functools.partial(kernel, n, exchange, nx),
        out_shape=jax.ShapeDtypeStruct(shape, f32),
        in_specs=[pl.BlockSpec(memory_space=pl.ANY)] * 2,
        out_specs=pl.BlockSpec(memory_space=pltpu.VMEM),
        scratch_shapes=scratch,
        compiler_params=pltpu.CompilerParams(
            collective_id=0, has_side_effects=True, vmem_limit_bytes=127 * 512 * 1024
        ),
    )(velocity.reshape(3 * CZ * YH, nx), jnp.asarray(constants()))
    if exchange:
        return result
    parts = result.reshape(4, n, pixels).transpose(1, 0, 2).astype(bf16)
    parts = lax.all_to_all(parts, "slab", 0, 0, tiled=True).astype(f32)
    depth = parts[:, 3]
    before = jnp.exp(-(jnp.cumsum(depth, axis=0) - depth))
    cover = 1.0 - jnp.exp(-depth)
    colours = jnp.sum(0.5 * before[:, None] * (cover[:, None] + parts[:, :3]), axis=0)
    return jnp.concatenate([colours, (1.0 - jnp.exp(-jnp.sum(depth, axis=0)))[None]], axis=0)


def solution(mesh):
    return jax.shard_map(
        per_device, mesh=mesh, in_specs=(P(None, "slab", None, None),), out_specs=P(None, "slab"), check_vma=False
    )
```

```python
import functools

import jax
import jax.numpy as jnp
import ml_dtypes
import numpy as np
from jax import lax
from jax.experimental import pallas as pl
from jax.experimental.pallas import tpu as pltpu
from jax.sharding import PartitionSpec as P

MESH = pl.DeviceIdType.MESH
opacity_gain = 5.0

smooth_taps = np.array([1, 4, 6, 4, 1]) / 16.0
slope_taps = np.array([1, -8, 0, 8, -1]) / 1.0
both_taps = np.convolve(smooth_taps, slope_taps)
CZ, YH, BAND = 4, 16, 8
KEEP = YH - 4
FIELDS = 6
LANE = 128
SIDE = 96
CHUNK = 1024
TILE = 512
CELL = 256
FLIGHT = 4


def halo_row(component, plane, row):
    below = plane < 0
    source = plane + CZ if below else plane - CZ
    spec, band = (0, 32) if below else (SIDE + 64, SIDE)
    near = source - 2 if below else source
    if component < 2 and 2 <= row < 2 + BAND:
        return band + 32 * component + source * BAND + row - 2
    assert component != 1 and 0 <= near < 2
    if component == 0:
        return spec + near * 4 + (row if row < 2 else row - BAND)
    return spec + 8 + near * KEEP + row


def weights():
    send = np.zeros((128, 192))
    own = np.zeros((FIELDS * 32, 192))
    halo = np.zeros((FIELDS * 32, 192))

    def put(at, component, source, row):
        for b in range(5):
            send[at, component * 64 + source * YH + row + b] += smooth_taps[b]

    for component in range(2):
        for source in range(CZ):
            for r in range(BAND):
                put(32 + 32 * component + source * BAND + r, component, source, r + 2)
    for start, planes in ((0, (2, 3)), (96, (0, 1))):
        for near, source in enumerate(planes):
            for i, row in enumerate((0, 1, 10, 11)):
                put(start + near * 4 + i, 0, source, row)
            for row in range(KEEP):
                put(start + 8 + near * KEEP + row, 2, source, row)

    def term(field, component, z_taps, y_slope, sign):
        y_own = both_taps if y_slope else smooth_taps
        y_halo = slope_taps if y_slope else np.ones(1)
        for p in range(CZ):
            for r in range(BAND):
                at = field * 32 + p * BAND + r
                for a, wz in enumerate(z_taps):
                    plane = p + a - len(z_taps) // 2
                    if wz == 0:
                        continue
                    if 0 <= plane < CZ:
                        for b, wy in enumerate(y_own):
                            row = r + 4 + b - len(y_own) // 2
                            own[at, component * 64 + plane * YH + row] += sign * wz * wy / 16.0
                    else:
                        for b, wy in enumerate(y_halo):
                            if wy:
                                row = r + 2 + b - len(y_halo) // 2
                                halo[at, halo_row(component, plane, row)] += sign * wz * wy / 16.0

    term(0, 2, smooth_taps, True, 1.0)
    term(0, 1, both_taps, False, -1.0)
    term(1, 0, both_taps, False, 1.0)
    term(2, 0, smooth_taps, True, 1.0)
    for k in range(3):
        term(3 + k, k, smooth_taps, False, 1.0)
    full = np.concatenate([send, own, halo], axis=0)
    rounded = full.astype(ml_dtypes.bfloat16)
    assert np.all(rounded.astype(np.float64) == full)
    return rounded


def band(taps):
    matrix = np.zeros((CELL + 2 * LANE, CELL))
    for j in range(CELL):
        for o, tap in enumerate(taps):
            matrix[LANE + j + o - 2, j] = tap
    return matrix


def constants():
    zy = np.pad(weights(), ((0, 0), (0, CELL - 192)))
    along_x = np.concatenate([band(16.0 * smooth_taps), band(slope_taps)], axis=0)
    return np.concatenate([zy, along_x.astype(ml_dtypes.bfloat16)], axis=0)


def dot(a, b):
    return jnp.dot(a, b, preferred_element_type=jnp.float32)


def kernel(n, exchange, nx, raw_hbm, mats_hbm, out, raw, mats, even, send, halo, fields, *rest):
    if exchange:
        staged, outbox, inbox, in_s, up_s, up_r, down_s, down_r, out_s, in_r = rest
    else:
        in_s, up_s, up_r, down_s, down_r = rest
    me = lax.axis_index("slab")
    up, down = lax.rem(me + 1, n), lax.rem(me + n - 1, n)
    barrier = pltpu.get_barrier_semaphore()
    chunks, tiles, cells = nx // CHUNK, nx // TILE, nx // CELL

    inward = [pltpu.make_async_copy(mats_hbm, mats, in_s.at[0])]
    for i, (first, width, at) in enumerate((
        (nx - CELL - LANE, LANE + CELL, 0),
        (0, CHUNK, LANE + CELL),
        (CHUNK, nx - CELL - CHUNK, LANE + CELL + CHUNK),
        (nx - CELL, LANE, LANE + nx),
    )):
        inward.append(pltpu.make_async_copy(
            raw_hbm.at[:, pl.ds(first, width)], raw.at[:, pl.ds(at, width)], in_s.at[i + 1]))
    for copy in inward:
        copy.start()
    if exchange:
        def greet(hop, _):
            pl.semaphore_signal(barrier, inc=1, device_id=(lax.rem(me + hop, n),), device_id_type=MESH)
            return 0

        lax.fori_loop(1, n, greet, 0)
    else:
        for other in (up, down):
            pl.semaphore_signal(barrier, inc=1, device_id=(other,), device_id_type=MESH)

    def halo_copies(k):
        lanes = pl.ds(pl.multiple_of(k * TILE, TILE), TILE)
        return (
            pltpu.make_async_remote_copy(
                src_ref=send.at[pl.ds(0, SIDE), lanes], dst_ref=halo.at[pl.ds(0, SIDE), lanes],
                send_sem=up_s.at[k], recv_sem=up_r.at[k], device_id=(up,), device_id_type=MESH),
            pltpu.make_async_remote_copy(
                src_ref=send.at[pl.ds(32, SIDE), lanes], dst_ref=halo.at[pl.ds(SIDE, SIDE), lanes],
                send_sem=down_s.at[k], recv_sem=down_r.at[k], device_id=(down,), device_id_type=MESH),
        )

    def to_send(k, _):
        first = pl.multiple_of(k * TILE, TILE)

        @pl.when(k == 2)
        def _():
            for copy in inward[3:]:
                copy.wait()

        for cell in range(TILE // CELL):
            at = pl.multiple_of(first + cell * CELL, CELL)
            lanes = pl.ds(at, CELL)
            part = dot(raw[:, pl.ds(at, CELL + 2 * LANE)], mats[512:1024, :]).astype(jnp.bfloat16)
            even[:, lanes] = part
            send[:, lanes] = dot(mats[0:128, 0:192], part).astype(jnp.bfloat16)

        @pl.when(k == 0)
        def _():
            pl.semaphore_wait(barrier, n - 1 if exchange else 2)

        @pl.when(k < FLIGHT)
        def _():
            for copy in halo_copies(k):
                copy.start()

        return 0

    for copy in inward[:3]:
        copy.wait()
    lax.fori_loop(0, tiles, to_send, 0)

    def add_halo(k, _):
        first = pl.multiple_of(k * CELL, CELL)
        lanes = pl.ds(first, CELL)
        total = dot(mats[128:320, 0:192], even[:, lanes]) + dot(mats[320:512, 0:192], halo[:, lanes])
        fields[:, pl.ds(first + LANE, CELL)] = total

        @pl.when(first == 0)
        def _():
            fields[128:192, nx + LANE:nx + 2 * LANE] = total[128:192, 0:LANE]

        @pl.when(first == nx - CELL)
        def _():
            fields[128:192, 0:LANE] = total[128:192, CELL - LANE:CELL]

        return 0

    scale = opacity_gain / (144.0 * CZ * n)
    per_chunk = CHUNK // CELL

    def shade(k, _):
        first = pl.multiple_of(lax.rem(k + 1, cells) * CELL, CELL)
        slopes = dot(fields[128:192, pl.ds(first, CELL + 2 * LANE)].astype(jnp.bfloat16), mats[1024:1536, :])
        through = None
        for p in range(CZ):
            def centre(field):
                return fields[field * 32 + p * BAND:field * 32 + (p + 1) * BAND, pl.ds(first + LANE, CELL)]

            def slope(field):
                return slopes[(field - 4) * 32 + p * BAND:(field - 4) * 32 + (p + 1) * BAND]

            curl = centre(0)
            square = curl * curl
            curl = centre(1) - slope(5)
            square += curl * curl
            curl = slope(4) - centre(2)
            density = (square + curl * curl) * scale
            left = jnp.exp(-density)
            tinted = [jnp.tanh(centre(3 + q)) for q in range(3)]
            if through is None:
                weight = 1.0 - left
                through, depth = left, density
                sums = [weight * u for u in tinted]
            else:
                weight = through * (1.0 - left)
                through, depth = through * left, depth + density
                sums = [s + weight * u for s, u in zip(sums, tinted)]
        for q, part in enumerate(sums + [depth]):
            if not exchange:
                out[q, :, pl.ds(pl.multiple_of(k * CELL, CELL), CELL)] = part
                continue
            for j in range(CELL // LANE):
                row = q * 8 + lax.rem(k, per_chunk) * (CELL // LANE) + j
                staged[pl.ds(pl.multiple_of(row * BAND, BAND), BAND), :] = part[:, j * LANE:(j + 1) * LANE]
        return 0

    per_tile = TILE // CELL

    def one_tile(k, _):
        for copy in halo_copies(k):
            copy.wait_recv()

        @pl.when(k + FLIGHT < tiles)
        def _():
            for copy in halo_copies(k):
                copy.wait_send()
            for copy in halo_copies(k + FLIGHT):
                copy.start()

        lax.fori_loop(k * per_tile, (k + 1) * per_tile, add_halo, 0)
        return 0

    def one_chunk(c, _):
        ready = CHUNK // TILE
        lax.fori_loop(jnp.where(c == 0, 0, c * ready + 1), jnp.minimum((c + 1) * ready + 1, tiles), one_tile, 0)
        lax.fori_loop(c * per_chunk, (c + 1) * per_chunk, shade, 0)
        if not exchange:
            return 0
        for r in range(BAND):
            outbox[c * BAND + r] = staged[pl.ds(r, 32, stride=BAND), :].astype(jnp.bfloat16)

        def post(r, _):
            owner = r * chunks + c

            @pl.when(owner != me)
            def _():
                pltpu.make_async_remote_copy(
                    src_ref=outbox.at[c * BAND + r], dst_ref=inbox.at[me], send_sem=out_s.at[owner],
                    recv_sem=in_r.at[me], device_id=(owner,), device_id_type=MESH).start()

            @pl.when(owner == me)
            def _():
                inbox[me] = outbox[c * BAND + r]

            return 0

        lax.fori_loop(0, BAND, post, 0)
        return 0

    lax.fori_loop(0, chunks, one_chunk, 0)

    if exchange:
        def arrived(hop, _):
            source = lax.rem(me + hop, n)
            pltpu.make_async_remote_copy(
                src_ref=outbox.at[0], dst_ref=inbox.at[source], send_sem=out_s.at[source],
                recv_sem=in_r.at[source], device_id=(source,), device_id_type=MESH).wait_recv()
            return 0

        lax.fori_loop(1, n, arrived, 0)
        through = jnp.ones((8, LANE), jnp.float32)
        total = [jnp.zeros((8, LANE), jnp.float32) for _ in range(3)]
        for s in range(n):
            block = inbox[s].astype(jnp.float32)
            left = jnp.exp(-block[24:32])
            half = 0.5 * through
            cover = 1.0 - left
            total = [t + half * (cover + block[q * 8:q * 8 + 8]) for q, t in enumerate(total)]
            through = through * left
        total.append(1.0 - through)
        for q, value in enumerate(total):
            for j in range(8):
                out[q:q + 1, pl.ds(j * LANE, LANE)] = value[j:j + 1, :]

        def left_home(hop, _):
            other = lax.rem(me + hop, n)
            pltpu.make_async_remote_copy(
                src_ref=outbox.at[0], dst_ref=inbox.at[me], send_sem=out_s.at[other],
                recv_sem=in_r.at[me], device_id=(other,), device_id_type=MESH).wait_send()
            return 0

        lax.fori_loop(1, n, left_home, 0)
    for k in range(tiles - FLIGHT, tiles):
        for copy in halo_copies(k):
            copy.wait_send()


def per_device(velocity):
    n = lax.axis_size("slab")
    nx = velocity.shape[3]
    pixels = BAND * nx // n
    exchange = pixels == CHUNK
    tiles = nx // TILE
    bf16, f32 = jnp.bfloat16, jnp.float32
    scratch = [
        pltpu.VMEM((192, nx + 2 * LANE), bf16),
        pltpu.VMEM((512 + 2 * (CELL + 2 * LANE), CELL), bf16),
        pltpu.VMEM((192, nx), bf16),
        pltpu.VMEM((128, nx), bf16),
        pltpu.VMEM((2 * SIDE, nx), bf16),
        pltpu.VMEM((FIELDS * 32, nx + 2 * LANE), f32),
    ]
    if exchange:
        scratch += [
            pltpu.VMEM((32 * BAND, LANE), f32),
            pltpu.VMEM((n, 32, LANE), bf16),
            pltpu.VMEM((n, 32, LANE), bf16),
        ]
    scratch += [pltpu.SemaphoreType.DMA((5,))]
    scratch += [pltpu.SemaphoreType.DMA((tiles,))] * 4
    if exchange:
        scratch += [pltpu.SemaphoreType.DMA((n,))] * 2
    shape = (4, pixels) if exchange else (4, BAND, nx)
    result = pl.pallas_call(
        functools.partial(kernel, n, exchange, nx),
        out_shape=jax.ShapeDtypeStruct(shape, f32),
        in_specs=[pl.BlockSpec(memory_space=pl.ANY)] * 2,
        out_specs=pl.BlockSpec(memory_space=pltpu.VMEM),
        scratch_shapes=scratch,
        compiler_params=pltpu.CompilerParams(
            collective_id=0, has_side_effects=True, vmem_limit_bytes=127 * 512 * 1024
        ),
    )(velocity.reshape(3 * CZ * YH, nx), jnp.asarray(constants()))
    if exchange:
        return result
    parts = result.reshape(4, n, pixels).transpose(1, 0, 2).astype(bf16)
    parts = lax.all_to_all(parts, "slab", 0, 0, tiled=True).astype(f32)
    depth = parts[:, 3]
    before = jnp.exp(-(jnp.cumsum(depth, axis=0) - depth))
    cover = 1.0 - jnp.exp(-depth)
    colours = jnp.sum(0.5 * before[:, None] * (cover[:, None] + parts[:, :3]), axis=0)
    return jnp.concatenate([colours, (1.0 - jnp.exp(-jnp.sum(depth, axis=0)))[None]], axis=0)


def solution(mesh):
    return jax.shard_map(
        per_device, mesh=mesh, in_specs=(P(None, "slab", None, None),), out_specs=P(None, "slab"), check_vma=False
    )
```

```python
import functools

import jax
import jax.numpy as jnp
import ml_dtypes
import numpy as np
from jax import lax
from jax.experimental import pallas as pl
from jax.experimental.pallas import tpu as pltpu
from jax.sharding import PartitionSpec as P

MESH = pl.DeviceIdType.MESH
opacity_gain = 5.0

smooth_taps = np.array([1, 4, 6, 4, 1]) / 16.0
slope_taps = np.array([1, -8, 0, 8, -1]) / 1.0
both_taps = np.convolve(smooth_taps, slope_taps)
CZ, YH, BAND = 4, 16, 8
KEEP = YH - 4
FIELDS = 6
LANE = 128
SIDE = 96
CHUNK = 1024
TILE = 512
CELL = 256
FLIGHT = 4


def halo_row(component, plane, row):
    below = plane < 0
    source = plane + CZ if below else plane - CZ
    spec, band = (0, 32) if below else (SIDE + 64, SIDE)
    near = source - 2 if below else source
    if component < 2 and 2 <= row < 2 + BAND:
        return band + 32 * component + source * BAND + row - 2
    assert component != 1 and 0 <= near < 2
    if component == 0:
        return spec + near * 4 + (row if row < 2 else row - BAND)
    return spec + 8 + near * KEEP + row


def weights():
    send = np.zeros((128, 192))
    own = np.zeros((FIELDS * 32, 192))
    halo = np.zeros((FIELDS * 32, 192))

    def put(at, component, source, row):
        for b in range(5):
            send[at, component * 64 + source * YH + row + b] += smooth_taps[b]

    for component in range(2):
        for source in range(CZ):
            for r in range(BAND):
                put(32 + 32 * component + source * BAND + r, component, source, r + 2)
    for start, planes in ((0, (2, 3)), (96, (0, 1))):
        for near, source in enumerate(planes):
            for i, row in enumerate((0, 1, 10, 11)):
                put(start + near * 4 + i, 0, source, row)
            for row in range(KEEP):
                put(start + 8 + near * KEEP + row, 2, source, row)

    def term(field, component, z_taps, y_slope, sign):
        y_own = both_taps if y_slope else smooth_taps
        y_halo = slope_taps if y_slope else np.ones(1)
        for p in range(CZ):
            for r in range(BAND):
                at = field * 32 + p * BAND + r
                for a, wz in enumerate(z_taps):
                    plane = p + a - len(z_taps) // 2
                    if wz == 0:
                        continue
                    if 0 <= plane < CZ:
                        for b, wy in enumerate(y_own):
                            row = r + 4 + b - len(y_own) // 2
                            own[at, component * 64 + plane * YH + row] += sign * wz * wy / 16.0
                    else:
                        for b, wy in enumerate(y_halo):
                            if wy:
                                row = r + 2 + b - len(y_halo) // 2
                                halo[at, halo_row(component, plane, row)] += sign * wz * wy / 16.0

    term(0, 2, smooth_taps, True, 1.0)
    term(0, 1, both_taps, False, -1.0)
    term(1, 0, both_taps, False, 1.0)
    term(2, 0, smooth_taps, True, 1.0)
    for k in range(3):
        term(3 + k, k, smooth_taps, False, 1.0)
    full = np.concatenate([send, own, halo], axis=0)
    rounded = full.astype(ml_dtypes.bfloat16)
    assert np.all(rounded.astype(np.float64) == full)
    return rounded


def band(taps):
    matrix = np.zeros((CELL + 2 * LANE, CELL))
    for j in range(CELL):
        for o, tap in enumerate(taps):
            matrix[LANE + j + o - 2, j] = tap
    return matrix


def constants():
    zy = np.pad(weights(), ((0, 0), (0, CELL - 192)))
    along_x = np.concatenate([band(16.0 * smooth_taps), band(slope_taps)], axis=0)
    return np.concatenate([zy, along_x.astype(ml_dtypes.bfloat16)], axis=0)


def dot(a, b):
    return jnp.dot(a, b, preferred_element_type=jnp.float32)


def kernel(n, exchange, nx, raw_hbm, mats_hbm, out, raw, mats, even, send, halo, fields, *rest):
    if exchange:
        staged, outbox, inbox, in_s, up_s, up_r, down_s, down_r, out_s, in_r = rest
    else:
        in_s, up_s, up_r, down_s, down_r = rest
    me = lax.axis_index("slab")
    up, down = lax.rem(me + 1, n), lax.rem(me + n - 1, n)
    barrier = pltpu.get_barrier_semaphore()
    chunks, tiles, cells = nx // CHUNK, nx // TILE, nx // CELL

    inward = [pltpu.make_async_copy(mats_hbm, mats, in_s.at[0])]
    for i, (first, width, at) in enumerate((
        (nx - CELL - LANE, LANE + CELL, 0),
        (0, CHUNK, LANE + CELL),
        (CHUNK, nx - CELL - CHUNK, LANE + CELL + CHUNK),
        (nx - CELL, LANE, LANE + nx),
    )):
        inward.append(pltpu.make_async_copy(
            raw_hbm.at[:, pl.ds(first, width)], raw.at[:, pl.ds(at, width)], in_s.at[i + 1]))
    for copy in inward:
        copy.start()
    if exchange:
        def greet(hop, _):
            pl.semaphore_signal(barrier, inc=1, device_id=(lax.rem(me + hop, n),), device_id_type=MESH)
            return 0

        lax.fori_loop(1, n, greet, 0)
    else:
        for other in (up, down):
            pl.semaphore_signal(barrier, inc=1, device_id=(other,), device_id_type=MESH)

    def halo_copies(k):
        return (
            pltpu.make_async_remote_copy(
                src_ref=send.at[k, pl.ds(0, SIDE)], dst_ref=halo.at[k, pl.ds(0, SIDE)],
                send_sem=up_s.at[k], recv_sem=up_r.at[k], device_id=(up,), device_id_type=MESH),
            pltpu.make_async_remote_copy(
                src_ref=send.at[k, pl.ds(32, SIDE)], dst_ref=halo.at[k, pl.ds(SIDE, SIDE)],
                send_sem=down_s.at[k], recv_sem=down_r.at[k], device_id=(down,), device_id_type=MESH),
        )

    def to_send(k, _):
        first = pl.multiple_of(k * TILE, TILE)

        @pl.when(k == 2)
        def _():
            for copy in inward[3:]:
                copy.wait()

        for cell in range(TILE // CELL):
            at = pl.multiple_of(first + cell * CELL, CELL)
            lanes = pl.ds(at, CELL)
            part = dot(raw[:, pl.ds(at, CELL + 2 * LANE)], mats[512:1024, :]).astype(jnp.bfloat16)
            even[:, lanes] = part
            send[k, :, cell * CELL:(cell + 1) * CELL] = dot(mats[0:128, 0:192], part).astype(jnp.bfloat16)

        @pl.when(k == 0)
        def _():
            pl.semaphore_wait(barrier, n - 1 if exchange else 2)

        @pl.when(k < FLIGHT)
        def _():
            for copy in halo_copies(k):
                copy.start()

        return 0

    for copy in inward[:3]:
        copy.wait()
    lax.fori_loop(0, tiles, to_send, 0)

    def add_halo(tile, cell):
        first = pl.multiple_of(tile * TILE + cell * CELL, CELL)
        lanes = pl.ds(first, CELL)
        arrived_cell = halo[tile, :, cell * CELL:(cell + 1) * CELL]
        total = dot(mats[128:320, 0:192], even[:, lanes]) + dot(mats[320:512, 0:192], arrived_cell)
        fields[:, pl.ds(first + LANE, CELL)] = total

        @pl.when(first == 0)
        def _():
            fields[128:192, nx + LANE:nx + 2 * LANE] = total[128:192, 0:LANE]

        @pl.when(first == nx - CELL)
        def _():
            fields[128:192, 0:LANE] = total[128:192, CELL - LANE:CELL]

    scale = opacity_gain / (144.0 * CZ * n)
    per_chunk = CHUNK // CELL

    def shade(k, _):
        first = pl.multiple_of(lax.rem(k + 1, cells) * CELL, CELL)
        slopes = dot(fields[128:192, pl.ds(first, CELL + 2 * LANE)].astype(jnp.bfloat16), mats[1024:1536, :])
        through = None
        for p in range(CZ):
            def centre(field):
                return fields[field * 32 + p * BAND:field * 32 + (p + 1) * BAND, pl.ds(first + LANE, CELL)]

            def slope(field):
                return slopes[(field - 4) * 32 + p * BAND:(field - 4) * 32 + (p + 1) * BAND]

            curl = centre(0)
            square = curl * curl
            curl = centre(1) - slope(5)
            square += curl * curl
            curl = slope(4) - centre(2)
            density = (square + curl * curl) * scale
            left = jnp.exp(-density)
            tinted = [jnp.tanh(centre(3 + q)) for q in range(3)]
            if through is None:
                weight = 1.0 - left
                through, depth = left, density
                sums = [weight * u for u in tinted]
            else:
                weight = through * (1.0 - left)
                through, depth = through * left, depth + density
                sums = [s + weight * u for s, u in zip(sums, tinted)]
        for q, part in enumerate(sums + [depth]):
            if not exchange:
                out[q, :, pl.ds(pl.multiple_of(k * CELL, CELL), CELL)] = part
                continue
            for j in range(CELL // LANE):
                row = q * 8 + lax.rem(k, per_chunk) * (CELL // LANE) + j
                staged[pl.ds(pl.multiple_of(row * BAND, BAND), BAND), :] = part[:, j * LANE:(j + 1) * LANE]
        return 0

    def one_tile(k, _):
        for copy in halo_copies(k):
            copy.wait_recv()

        @pl.when(k + FLIGHT < tiles)
        def _():
            for copy in halo_copies(k):
                copy.wait_send()
            for copy in halo_copies(k + FLIGHT):
                copy.start()

        for cell in range(TILE // CELL):
            add_halo(k, cell)
        return 0

    def one_chunk(c, _):
        ready = CHUNK // TILE
        lax.fori_loop(jnp.where(c == 0, 0, c * ready + 1), jnp.minimum((c + 1) * ready + 1, tiles), one_tile, 0)
        lax.fori_loop(c * per_chunk, (c + 1) * per_chunk, shade, 0)
        if not exchange:
            return 0
        for r in range(BAND):
            outbox[c * BAND + r] = staged[pl.ds(r, 32, stride=BAND), :].astype(jnp.bfloat16)

        def post(i, _):
            r = lax.rem(i + me // chunks, BAND)
            owner = r * chunks + c

            @pl.when(owner != me)
            def _():
                pltpu.make_async_remote_copy(
                    src_ref=outbox.at[c * BAND + r], dst_ref=inbox.at[me], send_sem=out_s.at[owner],
                    recv_sem=in_r.at[me], device_id=(owner,), device_id_type=MESH).start()

            @pl.when(owner == me)
            def _():
                inbox[me] = outbox[c * BAND + r]

            return 0

        lax.fori_loop(0, BAND, post, 0)
        return 0

    lax.fori_loop(0, chunks, one_chunk, 0)

    if exchange:
        def arrived(hop, _):
            source = lax.rem(me + hop, n)
            pltpu.make_async_remote_copy(
                src_ref=outbox.at[0], dst_ref=inbox.at[source], send_sem=out_s.at[source],
                recv_sem=in_r.at[source], device_id=(source,), device_id_type=MESH).wait_recv()
            return 0

        lax.fori_loop(1, n, arrived, 0)
        through = jnp.ones((8, LANE), jnp.float32)
        total = [jnp.zeros((8, LANE), jnp.float32) for _ in range(3)]
        for s in range(n):
            block = inbox[s].astype(jnp.float32)
            left = jnp.exp(-block[24:32])
            half = 0.5 * through
            cover = 1.0 - left
            total = [t + half * (cover + block[q * 8:q * 8 + 8]) for q, t in enumerate(total)]
            through = through * left
        total.append(1.0 - through)
        for q, value in enumerate(total):
            for j in range(8):
                out[q:q + 1, pl.ds(j * LANE, LANE)] = value[j:j + 1, :]

        def left_home(hop, _):
            other = lax.rem(me + hop, n)
            pltpu.make_async_remote_copy(
                src_ref=outbox.at[0], dst_ref=inbox.at[me], send_sem=out_s.at[other],
                recv_sem=in_r.at[me], device_id=(other,), device_id_type=MESH).wait_send()
            return 0

        lax.fori_loop(1, n, left_home, 0)
    for k in range(tiles - FLIGHT, tiles):
        for copy in halo_copies(k):
            copy.wait_send()


def per_device(velocity):
    n = lax.axis_size("slab")
    nx = velocity.shape[3]
    pixels = BAND * nx // n
    exchange = pixels == CHUNK
    tiles = nx // TILE
    bf16, f32 = jnp.bfloat16, jnp.float32
    scratch = [
        pltpu.VMEM((192, nx + 2 * LANE), bf16),
        pltpu.VMEM((512 + 2 * (CELL + 2 * LANE), CELL), bf16),
        pltpu.VMEM((192, nx), bf16),
        pltpu.VMEM((tiles, 128, TILE), bf16),
        pltpu.VMEM((tiles, 2 * SIDE, TILE), bf16),
        pltpu.VMEM((FIELDS * 32, nx + 2 * LANE), f32),
    ]
    if exchange:
        scratch += [
            pltpu.VMEM((32 * BAND, LANE), f32),
            pltpu.VMEM((n, 32, LANE), bf16),
            pltpu.VMEM((n, 32, LANE), bf16),
        ]
    scratch += [pltpu.SemaphoreType.DMA((5,))]
    scratch += [pltpu.SemaphoreType.DMA((tiles,))] * 4
    if exchange:
        scratch += [pltpu.SemaphoreType.DMA((n,))] * 2
    shape = (4, pixels) if exchange else (4, BAND, nx)
    result = pl.pallas_call(
        functools.partial(kernel, n, exchange, nx),
        out_shape=jax.ShapeDtypeStruct(shape, f32),
        in_specs=[pl.BlockSpec(memory_space=pl.ANY)] * 2,
        out_specs=pl.BlockSpec(memory_space=pltpu.VMEM),
        scratch_shapes=scratch,
        compiler_params=pltpu.CompilerParams(
            collective_id=0, has_side_effects=True, vmem_limit_bytes=53 * 1024 * 1024
        ),
    )(velocity.reshape(3 * CZ * YH, nx), jnp.asarray(constants()))
    if exchange:
        return result
    parts = result.reshape(4, n, pixels).transpose(1, 0, 2).astype(bf16)
    parts = lax.all_to_all(parts, "slab", 0, 0, tiled=True).astype(f32)
    depth = parts[:, 3]
    before = jnp.exp(-(jnp.cumsum(depth, axis=0) - depth))
    cover = 1.0 - jnp.exp(-depth)
    colours = jnp.sum(0.5 * before[:, None] * (cover[:, None] + parts[:, :3]), axis=0)
    return jnp.concatenate([colours, (1.0 - jnp.exp(-jnp.sum(depth, axis=0)))[None]], axis=0)


def solution(mesh):
    return jax.shard_map(
        per_device, mesh=mesh, in_specs=(P(None, "slab", None, None),), out_specs=P(None, "slab"), check_vma=False
    )
```
